256 devices in a mesh: tm: 4 (over z_hi), feed: 64 (over y, z_lo, x, core).
Axes of the slice: x: 4, y: 4, z: 8 (z_hi: 4, z_lo: 2; z = z_hi * 2 + z_lo), core: 2. Of those that a mesh axis runs over, the one named last changes fastest.
Arguments:
- voltages: int32 [1024, 524288], P('feed', 'tm'), may hold values from -128 to 127
- window: float32 [4, 2048], replicated, may hold values from -0.04 to 0.04
- first_channel: int32 [1], replicated, may hold values from 0 to 512
Outputs:
- visibility: bfloat16 [1024, 512, 1024], P('tm', 'feed')
The draws below stay inside these ranges and needn't reach their ends.
Inputs may be any that keep to these rules, and one draw needn't show every extreme that they name: first_channel[0] + 512 <= 1024.
All inputs are finite; a program needn't handle non-finite values.
Results may differ from the reference program's by a relative error of at most 0.0071.
Values may be sent and summed in bfloat16 or wider, within the bound.
No kernel may reach another device: no remote copies, remote signals or barrier semaphores. Data moves between devices by JAX's collectives and lax.ppermute only.
A program may use at most 128 MiB of HBM per device.

```python
import math
import jax
import jax.numpy as jnp
from jax import lax

NFFT = 2048
TAPS = 4
INP_DEV = 16
SPEC_DEV = 64
INPUTS = 1024
CHANNELS = 512
SPECTRA = 256
SAMPLES = 524288
N_FEED = 64


def place_ends(values, stream_key, smallest, high):
    spot = [jax.random.randint(jax.random.fold_in(stream_key, axis), (), 0, length) for axis, length in enumerate(values.shape)]
    widest = values.shape.index(max(values.shape))
    next_to = spot[:widest] + [(spot[widest] + 1) % values.shape[widest]] + spot[widest + 1:]
    return values.at[tuple(spot)].set(smallest).at[tuple(next_to)].set(high)


def gaussian(own_key, shape, scale, reach, kind=jnp.bfloat16):
    values = scale * jax.random.normal(own_key, shape, jnp.float32)
    return jnp.clip(values, min=-reach, max=reach).astype(kind)


def setup_inputs(seed: int = 0) -> dict:
    seeds = jax.random.split(jax.random.key(seed), 4)
    return {
        "voltages": place_ends(jax.random.randint(seeds[0], (INPUTS, SAMPLES), -128, 128), jax.random.fold_in(seeds[0], 1), -128, 127).astype(jnp.int32),
        "window": gaussian(seeds[1], (TAPS, NFFT), 0.0068, 0.04, jnp.float32),
        "first_channel": jax.random.randint(seeds[2], (1,), 0, NFFT // 2 - CHANNELS + 1).astype(jnp.int32),
    }


def make_table(first_channel, frame_len, chan_count):
    sample_idx = lax.iota(jnp.int32, frame_len)
    chan_idx = first_channel[0].astype(jnp.int32) + lax.iota(jnp.int32, chan_count)
    phase_index = sample_idx[:, None] * chan_idx[None, :] % frame_len
    angles = phase_index.astype(jnp.float32) * jnp.float32(2.0 * math.pi / frame_len)
    norm_scale = jnp.float32(1.0 / math.sqrt(frame_len))
    return jnp.concatenate([jnp.cos(angles) * norm_scale, -jnp.sin(angles) * norm_scale], 1).astype(jnp.bfloat16)

def reference(voltages, window, first_channel):
    frames = voltages.reshape(N_FEED, INP_DEV, SPECTRA, NFFT)
    dft_table = make_table(first_channel, NFFT, CHANNELS)
    frame_phase = jnp.arange(SPECTRA, dtype=jnp.int32) % SPEC_DEV

    def one_block(raw_block):
        samples = raw_block.astype(jnp.float32)
        padded = jnp.concatenate([jnp.zeros((INP_DEV, TAPS - 1, NFFT), jnp.float32), samples], 1)
        own_sum = jnp.zeros((INP_DEV, SPECTRA, NFFT), jnp.float32)
        far_sum = jnp.zeros((INP_DEV, SPECTRA, NFFT), jnp.float32)
        for tap_index in range(TAPS):
            tap_term = window[tap_index][None, None, :] * padded[:, TAPS - 1 - tap_index:TAPS - 1 - tap_index + SPECTRA]
            is_local = (frame_phase >= tap_index)[None, :, None]
            own_sum = own_sum + jnp.where(is_local, tap_term, jnp.float32(0.0))
            far_sum = far_sum + jnp.where(is_local, jnp.float32(0.0), tap_term)
        far_round = lax.optimization_barrier(far_sum.astype(jnp.bfloat16))
        filtered = (own_sum + far_round.astype(jnp.float32)).astype(jnp.bfloat16)
        spectra = jnp.dot(filtered.reshape(INP_DEV * SPECTRA, NFFT), dft_table, preferred_element_type=jnp.float32)
        return spectra.astype(jnp.bfloat16).reshape(INP_DEV, SPECTRA, 2, CHANNELS)
    spectra_all = lax.map(one_block, frames).reshape(INPUTS, SPECTRA, 2, CHANNELS)
    by_channel = jnp.transpose(spectra_all, (3, 0, 1, 2))
    lower_mask = jnp.arange(INPUTS)[:, None] >= jnp.arange(INPUTS)[None, :]

    def one_channel(chan_data):
        stacked = chan_data.reshape(INPUTS, 2 * SPECTRA)
        swapped = jnp.stack([chan_data[:, :, 1], -chan_data[:, :, 0]], -1).reshape(INPUTS, 2 * SPECTRA)
        real_part = jnp.dot(stacked, stacked.T, preferred_element_type=jnp.float32)
        imag_part = jnp.dot(swapped, stacked.T, preferred_element_type=jnp.float32)
        packed = jnp.where(lower_mask, real_part, imag_part) / jnp.float32(SPECTRA)
        return packed.astype(jnp.bfloat16)
    visibility = lax.map(one_channel, by_channel)
    return jnp.transpose(visibility, (1, 0, 2))
```

```python
import functools
import math

import jax
import jax.numpy as jnp
from jax import lax
from jax.experimental import pallas as pl
from jax.experimental.pallas import tpu as pltpu
from jax.sharding import PartitionSpec as P

FRAME = 2048
TAPS = 4
INP = 16
SPEC = 64
INPUTS = 1024
N_TM = 4
N_FEED = 64
CH_DEV = 8
FRAME_BLOCK = 8
LANES = 256
COARSE = 32
FINE = FRAME // COARSE
ROWS = INPUTS // N_TM
PIECE = 2 * SPEC
MIB = 1 << 20


def params(mib):
    return pltpu.CompilerParams(vmem_limit_bytes=mib * MIB)


def ring(by):
    return [(i, (i + by) % N_TM) for i in range(N_TM)]


def to_right(x):
    return lax.ppermute(x, "tm", ring(1))


def to_left(x):
    return lax.ppermute(x, "tm", ring(-1))


def carry_kernel(v_ref, w_ref, out_ref):
    for head in range(TAPS - 1):
        for start in range(0, FRAME, LANES):
            total = jnp.zeros((INP, LANES), jnp.float32)
            for tap in range(head + 1, TAPS):
                at = (4 + head - tap) * FRAME + start
                total = total + w_ref[tap : tap + 1, start : start + LANES] * v_ref[
                    :, at : at + LANES
                ].astype(jnp.float32)
            out_ref[head * INP : (head + 1) * INP, start : start + LANES] = total.astype(jnp.bfloat16)


def carry(voltages, window):
    last = voltages.shape[1] // (4 * FRAME) - 1
    return pl.pallas_call(
        carry_kernel,
        grid=(1,),
        in_specs=[
            pl.BlockSpec((INP, 4 * FRAME), lambda g: (0, last)),
            pl.BlockSpec((TAPS, FRAME), lambda g: (0, 0)),
        ],
        out_specs=pl.BlockSpec(((TAPS - 1) * INP, FRAME), lambda g: (0, 0)),
        out_shape=jax.ShapeDtypeStruct(((TAPS - 1) * INP, FRAME), jnp.bfloat16),
        compiler_params=params(32),
        name="carry",
    )(voltages, window)


def filter_kernel(v_ref, w_ref, out_ref, head_ref, past):
    step = pl.program_id(0)

    @pl.when(step == 0)
    def _():
        past[...] = jnp.zeros_like(past)

    for start in range(0, FRAME, LANES):
        cols = slice(start, start + LANES)
        taps = [
            jnp.broadcast_to(w_ref[p : p + 1, cols], (INP, LANES)) for p in range(TAPS)
        ]
        seen = [past[p, :, cols] for p in range(TAPS - 1)]
        for k in range(FRAME_BLOCK):
            now = v_ref[:, k * FRAME + start : k * FRAME + start + LANES].astype(jnp.float32)
            total = taps[0] * now
            for p in range(1, TAPS):
                total = total + taps[p] * seen[p - 1]
            out_ref[k * INP : (k + 1) * INP, cols] = total.astype(jnp.bfloat16)
            if k < TAPS - 1:

                @pl.when(step == 0)
                def _():
                    head_ref[k * INP : (k + 1) * INP, cols] = total

            seen = [now] + seen[:-1]
        for p in range(TAPS - 1):
            past[p, :, cols] = seen[p]


def filter_own(voltages, window):
    steps = SPEC // FRAME_BLOCK
    head_rows = (TAPS - 1) * INP
    return pl.pallas_call(
        filter_kernel,
        grid=(steps,),
        in_specs=[
            pl.BlockSpec((INP, FRAME_BLOCK * FRAME), lambda g: (0, g)),
            pl.BlockSpec((TAPS, FRAME), lambda g: (0, 0)),
        ],
        out_specs=[
            pl.BlockSpec((FRAME_BLOCK * INP, FRAME), lambda g: (g, 0)),
            pl.BlockSpec((head_rows, FRAME), lambda g: (0, 0)),
        ],
        out_shape=[
            jax.ShapeDtypeStruct((SPEC * INP, FRAME), jnp.bfloat16),
            jax.ShapeDtypeStruct((head_rows, FRAME), jnp.float32),
        ],
        scratch_shapes=[pltpu.VMEM((TAPS - 1, INP, FRAME), jnp.float32)],
        compiler_params=params(32),
        name="own_filter",
    )(voltages, window)


def table_kernel(coarse_cos, coarse_sin, fine_cos, fine_sin, out_ref):
    half = fine_cos.shape[1] // 2
    for piece in range(2):
        cols = slice(piece * half, (piece + 1) * half)
        for a in range(COARSE):
            ac, as_ = coarse_cos[a : a + 1, cols], coarse_sin[a : a + 1, cols]
            bc, bs = fine_cos[:, cols], fine_sin[:, cols]
            rows = slice(a * FINE, (a + 1) * FINE)
            out_ref[piece, rows, :half] = (ac * bc - as_ * bs).astype(jnp.bfloat16)
            out_ref[piece, rows, half:] = (-(as_ * bc) - ac * bs).astype(jnp.bfloat16)


def table(first_channel, position, which):
    column = lax.iota(jnp.int32, N_FEED * N_TM)
    group = (position + column % N_TM) % N_TM
    channel = first_channel[0] + column // N_TM * CH_DEV + 2 * group + which

    def waves(samples):
        phase = samples[:, None] * channel[None, :] % FRAME
        angle = phase.astype(jnp.float32) * jnp.float32(2.0 * math.pi / FRAME)
        return jnp.cos(angle), jnp.sin(angle)

    scale = jnp.float32(1.0 / math.sqrt(FRAME))
    coarse = waves(FINE * lax.iota(jnp.int32, COARSE))
    fine = waves(lax.iota(jnp.int32, FINE))
    return pl.pallas_call(
        table_kernel,
        out_shape=jax.ShapeDtypeStruct((2, FRAME, N_FEED * N_TM), jnp.bfloat16),
        compiler_params=params(32),
        name="dft_table",
    )(coarse[0], coarse[1], fine[0] * scale, fine[1] * scale)


def dft_kernel(f_ref, head_ref, arrived_ref, t_ref, out_ref, fixed, wide, turned):
    head_rows = head_ref.shape[0]

    @pl.when(pl.program_id(0) == 0)
    def _():
        fixed[...] = (head_ref[...] + arrived_ref[...].astype(jnp.float32)).astype(jnp.bfloat16)

    first = jnp.dot(fixed[...], t_ref[0], preferred_element_type=jnp.float32)
    rest = jnp.dot(f_ref[head_rows:, :], t_ref[0], preferred_element_type=jnp.float32)
    for r in range(2):
        wide[r, :head_rows, :] = first[:, r * 128 : (r + 1) * 128]
        wide[r, head_rows:, :] = rest[:, r * 128 : (r + 1) * 128]
    for i in range(INP):
        rows = pl.ds(i, SPEC, stride=INP)
        both = jnp.concatenate([wide[0, rows, :], wide[1, rows, :]], 0)
        turned[pl.ds(i, 128, stride=INP), :] = both.T
    out_ref[...] = turned[...].astype(jnp.bfloat16).reshape(out_ref.shape)


def dft(filtered, head, arrived, dft_table):
    steps = dft_table.shape[0]
    whole = lambda g: (0, 0)
    return pl.pallas_call(
        dft_kernel,
        grid=(steps,),
        in_specs=[
            pl.BlockSpec(filtered.shape, whole),
            pl.BlockSpec(head.shape, whole),
            pl.BlockSpec(arrived.shape, whole),
            pl.BlockSpec((1, FRAME, 256), lambda g: (g, 0, 0)),
        ],
        out_specs=pl.BlockSpec((128, INP, PIECE), lambda g: (g, 0, 0)),
        out_shape=jax.ShapeDtypeStruct((steps * 128, INP, PIECE), jnp.bfloat16),
        scratch_shapes=[
            pltpu.VMEM(head.shape, jnp.bfloat16),
            pltpu.VMEM((2, SPEC * INP, 128), jnp.float32),
            pltpu.VMEM((128 * INP, PIECE), jnp.float32),
        ],
        compiler_params=params(48),
        name="dft",
    )(filtered, head, arrived, dft_table)


def correlate_kernel(row_ref, *refs):
    pieces, out_ref = refs[:N_TM], refs[N_TM]
    block = row_ref[0]
    at = pl.ds(pl.multiple_of(block * ROWS, ROWS), ROWS)
    mine = [piece[at, :] for piece in pieces]
    plain = jnp.concatenate(mine, 1)
    crossed = jnp.concatenate(
        [x for m in mine for x in (m[:, SPEC:], -m[:, :SPEC])], 1
    )
    scale = jnp.float32(1.0 / (SPEC * N_TM))
    contract = (((1,), (1,)), ((), ()))
    for other in range(N_TM):
        cols = slice(other * ROWS, (other + 1) * ROWS)
        left = jnp.where(other <= block, plain, crossed)
        right = jnp.concatenate([piece[cols, :] for piece in pieces], 1)
        part = lax.dot_general(left, right, contract, preferred_element_type=jnp.float32)
        out_ref[:, cols] = (part * scale).astype(jnp.bfloat16)
    part = lax.dot_general(crossed, plain, contract, preferred_element_type=jnp.float32)
    lower = lax.broadcasted_iota(jnp.int32, (ROWS, ROWS), 0) >= lax.broadcasted_iota(
        jnp.int32, (ROWS, ROWS), 1
    )
    both = jnp.where(lower, out_ref[:, at].astype(jnp.float32), part * scale)
    out_ref[:, at] = both.astype(jnp.bfloat16)


def correlate(block, pieces):
    vmem = pl.BlockSpec(memory_space=pltpu.VMEM)
    return pl.pallas_call(
        correlate_kernel,
        in_specs=[pl.BlockSpec(memory_space=pltpu.SMEM)] + [vmem] * N_TM,
        out_specs=vmem,
        out_shape=jax.ShapeDtypeStruct((ROWS, INPUTS), jnp.bfloat16),
        compiler_params=params(32),
        name="correlate",
    )(block.astype(jnp.int32).reshape(1), *pieces)


def gather_kernel(position_ref, *refs):
    planes, out_ref, wide = refs[:CH_DEV], refs[CH_DEV], refs[CH_DEV + 1]
    rows = planes[0].shape[0]
    for place in range(CH_DEV):
        channel = 2 * lax.rem(position_ref[0] + place // 2, N_TM) + place % 2
        for part in range(INPUTS // 128):
            cols = slice(part * 128, (part + 1) * 128)
            wide[part, pl.ds(channel, rows, stride=CH_DEV), :] = planes[place][:, cols].astype(
                jnp.float32
            )
    for part in range(INPUTS // 128):
        cols = slice(part * 128, (part + 1) * 128)
        out_ref[:, :, cols] = wide[part].astype(jnp.bfloat16).reshape(rows, CH_DEV, 128)


def gather_planes(position, planes):
    block = 64
    return pl.pallas_call(
        gather_kernel,
        grid=(ROWS // block,),
        in_specs=[pl.BlockSpec(memory_space=pltpu.SMEM)]
        + [pl.BlockSpec((block, INPUTS), lambda g: (g, 0))] * CH_DEV,
        out_specs=pl.BlockSpec((block, CH_DEV, INPUTS), lambda g: (g, 0, 0)),
        out_shape=jax.ShapeDtypeStruct((ROWS, CH_DEV, INPUTS), jnp.bfloat16),
        scratch_shapes=[pltpu.VMEM((INPUTS // 128, block * CH_DEV, 128), jnp.float32)],
        compiler_params=params(32),
        name="gather_planes",
    )(position.astype(jnp.int32).reshape(1), *planes)


def per_device(voltages, window, first_channel):
    position = lax.axis_index("tm")
    after, before = (position + 1) % N_TM, (position + N_TM - 1) % N_TM
    arrived = lax.ppermute(carry(voltages, window), "tm", [(i, i + 1) for i in range(N_TM - 1)])
    tables = [table(first_channel, position, which) for which in range(2)]
    filtered, head = filter_own(voltages, window)
    planes = [None] * CH_DEV
    for which in range(2):
        spectra = dft(filtered, head, arrived, tables[which])
        turned = lax.all_to_all(spectra, "feed", split_axis=0, concat_axis=0, tiled=True)
        turned = turned.reshape(N_FEED, N_TM, INP, PIECE)
        own = [turned[:, p].reshape(INPUTS, PIECE) for p in range(N_TM)]
        left_1, right_2 = to_right(own[1]), to_left(own[2])
        left_0, right_3 = to_right(own[0]), to_left(own[3])
        far_right, far_left = to_left(right_2), to_right(left_1)
        here = [own[0], left_1, right_3, far_right]
        there = [own[3], left_0, right_2, far_left]
        from_right = to_left(correlate(before, here))
        from_left = to_right(correlate(after, there))
        planes[0 + which] = correlate(position, here)
        planes[2 + which] = from_right
        planes[4 + which] = from_left
        planes[6 + which] = correlate(position, there)
    return gather_planes(position, planes)


def solution(mesh):
    in_specs = (P("feed", "tm"), P(), P())
    out_specs = P("tm", "feed", None)
    return jax.shard_map(
        per_device, mesh=mesh, in_specs=in_specs, out_specs=out_specs, check_vma=False
    )
```

```python
import functools
import math

import jax
import jax.numpy as jnp
from jax import lax
from jax.experimental import pallas as pl
from jax.experimental.pallas import tpu as pltpu
from jax.sharding import PartitionSpec as P

FRAME = 2048
TAPS = 4
INP = 16
SPEC = 64
INPUTS = 1024
N_TM = 4
N_FEED = 64
N_Z = 8
N_D = 32
CH_DEV = 8
FRAME_BLOCK = 8
DEPTH = 4
LANES = 256
COARSE = 32
FINE = FRAME // COARSE
ROWS = INPUTS // N_TM
PIECE = 2 * SPEC
BLOCK = (N_TM, N_D // N_TM, INP, PIECE)
EARLY = (2, 0, 5)
LATE = (1, 3, 4, 6, 7)
FAR = 2 * len(LATE)
MIB = 1 << 20


def in_hbm(x):
    return pltpu.with_memory_space_constraint(x, pltpu.HBM)


def params(mib):
    return pltpu.CompilerParams(vmem_limit_bytes=mib * MIB)


def place_of(tm, z_lo, d):
    return tm * N_FEED + (d // 8 * 2 + z_lo) * 8 + d % 8


def along_z(x, by):
    pairs = []
    for z in range(N_Z):
        to = (z + by) % N_Z
        for d in range(N_D):
            pairs.append((place_of(z // 2, z % 2, d), place_of(to // 2, to % 2, d)))
    return lax.ppermute(x, ("tm", "feed"), pairs)


def both_ways(left, right, by):
    return lax.optimization_barrier((along_z(left, -by), along_z(right, by)))


def turn(x):
    groups = [[place_of(0, z_lo, d) for d in range(N_D)] for z_lo in range(2)]
    return lax.all_to_all(
        x, "feed", split_axis=0, concat_axis=0, tiled=True, axis_index_groups=groups
    )


def carry_kernel(v_ref, w_ref, out_ref, held, sem):
    at = v_ref.shape[1] - (TAPS - 1) * FRAME
    copy = pltpu.make_async_copy(v_ref.at[:, pl.ds(at, (TAPS - 1) * FRAME)], held, sem)
    copy.start()
    copy.wait()
    for head in range(TAPS - 1):
        for start in range(0, FRAME, LANES):
            total = jnp.zeros((INP, LANES), jnp.float32)
            for tap in range(head + 1, TAPS):
                at = (TAPS - 1 + head - tap) * FRAME + start
                total = total + w_ref[tap : tap + 1, start : start + LANES] * held[
                    :, at : at + LANES
                ].astype(jnp.float32)
            out_ref[head * INP : (head + 1) * INP, start : start + LANES] = total.astype(jnp.bfloat16)


def carry(voltages, window):
    return pl.pallas_call(
        carry_kernel,
        in_specs=[
            pl.BlockSpec(memory_space=pltpu.HBM),
            pl.BlockSpec(memory_space=pltpu.VMEM),
        ],
        out_specs=pl.BlockSpec(memory_space=pltpu.VMEM),
        out_shape=jax.ShapeDtypeStruct(((TAPS - 1) * INP, FRAME), jnp.bfloat16),
        scratch_shapes=[
            pltpu.VMEM((INP, (TAPS - 1) * FRAME), jnp.int32),
            pltpu.SemaphoreType.DMA,
        ],
        compiler_params=params(8),
        name="carry",
    )(in_hbm(voltages), window)


def filter_kernel(v_ref, w_ref, out_ref, head_ref, held, past, sems):
    width = FRAME_BLOCK * FRAME
    steps = SPEC // FRAME_BLOCK

    def fetch(step):
        return pltpu.make_async_copy(
            v_ref.at[:, pl.ds(step * width, width)], held.at[step % DEPTH], sems.at[step % DEPTH]
        )

    for step in range(DEPTH - 1):
        fetch(step).start()
    past[...] = jnp.zeros_like(past)
    for step in range(steps):
        if step + DEPTH - 1 < steps:
            fetch(step + DEPTH - 1).start()
        fetch(step).wait()
        for start in range(0, FRAME, LANES):
            cols = slice(start, start + LANES)
            taps = [
                jnp.broadcast_to(w_ref[p : p + 1, cols], (INP, LANES)) for p in range(TAPS)
            ]
            seen = [past[p, :, cols] for p in range(TAPS - 1)]
            for k in range(FRAME_BLOCK):
                now = held[step % DEPTH, :, k * FRAME + start : k * FRAME + start + LANES].astype(
                    jnp.float32
                )
                total = taps[0] * now
                for p in range(1, TAPS):
                    total = total + taps[p] * seen[p - 1]
                row = (step * FRAME_BLOCK + k) * INP
                out_ref[row : row + INP, cols] = total.astype(jnp.bfloat16)
                if row < head_ref.shape[0]:
                    head_ref[row : row + INP, cols] = total
                seen = [now] + seen[:-1]
            for p in range(TAPS - 1):
                past[p, :, cols] = seen[p]


def filter_own(voltages, window):
    head_rows = (TAPS - 1) * INP
    vmem = pl.BlockSpec(memory_space=pltpu.VMEM)
    return pl.pallas_call(
        filter_kernel,
        in_specs=[pl.BlockSpec(memory_space=pltpu.HBM), vmem],
        out_specs=[vmem, vmem],
        out_shape=[
            jax.ShapeDtypeStruct((SPEC * INP, FRAME), jnp.bfloat16),
            jax.ShapeDtypeStruct((head_rows, FRAME), jnp.float32),
        ],
        scratch_shapes=[
            pltpu.VMEM((DEPTH, INP, FRAME_BLOCK * FRAME), jnp.int32),
            pltpu.VMEM((TAPS - 1, INP, FRAME), jnp.float32),
            pltpu.SemaphoreType.DMA((DEPTH,)),
        ],
        compiler_params=params(14),
        name="own_filter",
    )(in_hbm(voltages), window)


def table_kernel(coarse_cos, coarse_sin, fine_cos, fine_sin, out_ref):
    half = out_ref.shape[2] // 2
    for part in range(out_ref.shape[0]):
        cols = slice(part * half, (part + 1) * half)
        for a in range(COARSE):
            ac, as_ = coarse_cos[a : a + 1, cols], coarse_sin[a : a + 1, cols]
            bc, bs = fine_cos[:, cols], fine_sin[:, cols]
            rows = slice(a * FINE, (a + 1) * FINE)
            out_ref[part, rows, :half] = (ac * bc - as_ * bs).astype(jnp.bfloat16)
            out_ref[part, rows, half:] = (-(as_ * bc) - ac * bs).astype(jnp.bfloat16)


def table(first_channel, z):
    column = lax.iota(jnp.int32, N_D * FAR)
    runs = jnp.repeat(jnp.arange(2 * len(EARLY), dtype=jnp.int32), N_D)
    early, late = jnp.array(EARLY, jnp.int32), jnp.array(LATE, jnp.int32)
    d = jnp.concatenate([column // FAR, lax.iota(jnp.int32, N_D * 2 * len(EARLY)) % N_D])
    delta = jnp.concatenate([late[column % len(LATE)], early[runs // 2]])
    which = jnp.concatenate([column % FAR // len(LATE), runs % 2])
    group = (z + N_Z - delta) % N_Z
    feed = (d // 8 * 2 + group % 2) * 8 + d % 8
    channel = first_channel[0] + feed * CH_DEV + group // 2 * 2 + which

    def waves(samples):
        phase = samples[:, None] * channel[None, :] % FRAME
        angle = phase.astype(jnp.float32) * jnp.float32(2.0 * math.pi / FRAME)
        return jnp.cos(angle), jnp.sin(angle)

    scale = jnp.float32(1.0 / math.sqrt(FRAME))
    coarse = waves(FINE * lax.iota(jnp.int32, COARSE))
    fine = waves(lax.iota(jnp.int32, FINE))
    return pl.pallas_call(
        table_kernel,
        out_shape=jax.ShapeDtypeStruct((4, FRAME, N_D * N_Z), jnp.bfloat16),
        compiler_params=params(16),
        name="dft_table",
    )(coarse[0], coarse[1], fine[0] * scale, fine[1] * scale)


def dft_kernel(dests, f_ref, head_ref, arrived_ref, t_ref, *refs):
    outs, (fixed, wide, turned) = refs[:-3], refs[-3:]
    head_rows = head_ref.shape[0]
    fixed[...] = (head_ref[...] + arrived_ref[...].astype(jnp.float32)).astype(jnp.bfloat16)
    for part in range(t_ref.shape[0]):
        first = jnp.dot(fixed[...], t_ref[part], preferred_element_type=jnp.float32)
        rest = jnp.dot(f_ref[head_rows:, :], t_ref[part], preferred_element_type=jnp.float32)
        for r in range(2):
            wide[part, r, :head_rows, :] = first[:, r * 128 : (r + 1) * 128]
            wide[part, r, head_rows:, :] = rest[:, r * 128 : (r + 1) * 128]
    for part in range(t_ref.shape[0]):
        for i in range(INP):
            rows = pl.ds(i, SPEC, stride=INP)
            both = jnp.concatenate([wide[part, 0, rows, :], wide[part, 1, rows, :]], 0)
            turned[part, pl.ds(i, 128, stride=INP), :] = both.T
        for run in range(4):
            rows = slice(run * N_D * INP, (run + 1) * N_D * INP)
            block = turned[part, rows, :].astype(jnp.bfloat16).reshape(BLOCK)
            for n, (which, at) in enumerate(dests[part * 4 + run]):
                if outs[which].shape[0] == at + 2:
                    outs[which][at:] = block[2 * n : 2 * n + 2]
                else:
                    outs[which][at : at + 4] = block


def dft(filtered, head, arrived, dft_table, counts, dests):
    parts = dft_table.shape[0]
    vmem = pl.BlockSpec(memory_space=pltpu.VMEM)
    return pl.pallas_call(
        functools.partial(dft_kernel, dests),
        in_specs=[vmem] * 4,
        out_specs=[vmem] * len(counts),
        out_shape=[jax.ShapeDtypeStruct((count, *BLOCK[1:]), jnp.bfloat16) for count in counts],
        scratch_shapes=[
            pltpu.VMEM(head.shape, jnp.bfloat16),
            pltpu.VMEM((parts, 2, SPEC * INP, 128), jnp.float32),
            pltpu.VMEM((parts, 128 * INP, PIECE), jnp.float32),
        ],
        compiler_params=params(24),
        name="dft",
    )(filtered, head, arrived, dft_table)


def move_kernel(moves, n_in, *refs):
    ins, outs, sems = refs[:n_in], refs[n_in:-1], refs[-1]
    copies = [
        pltpu.make_async_copy(ins[i].at[src], outs[o].at[dst], sems.at[n])
        for n, (i, src, o, dst) in enumerate(moves)
    ]
    for copy in copies:
        copy.start()
    for copy in copies:
        copy.wait()


def move(arrays, shapes, moves):
    return pl.pallas_call(
        functools.partial(move_kernel, moves, len(arrays)),
        in_specs=[pl.BlockSpec(memory_space=pltpu.HBM)] * len(arrays),
        out_specs=[pl.BlockSpec(memory_space=pltpu.VMEM)] * len(shapes),
        out_shape=[jax.ShapeDtypeStruct(shape, jnp.bfloat16) for shape in shapes],
        scratch_shapes=[pltpu.SemaphoreType.DMA((len(moves),))],
        compiler_params=params(4),
        name="move",
    )(*[in_hbm(x) for x in arrays])


def correlate_kernel(layout, where_ref, *refs):
    arrays, (out_ref, x, sems) = refs[:-3], refs[-3:]
    z_lo = where_ref[1]
    copies = []
    for delta, parts in enumerate(layout):
        step, odd = divmod(delta, 2)
        half = lax.rem(z_lo + odd, 2)
        slot = lax.rem(step + z_lo * odd, N_TM)
        for which, at, to, count in parts:
            if len(arrays[which].shape) == 5:
                source = arrays[which].at[:, :, at]
            else:
                source = arrays[which].at[pl.ds(at, count)]
            goal = x.at[slot, pl.ds(to, count), half]
            copies.append(pltpu.make_async_copy(source, goal, sems.at[len(copies)]))
    for copy in copies:
        copy.start()
    for copy in copies:
        copy.wait()
    scale = jnp.float32(1.0 / (SPEC * N_TM))
    contract = (((1,), (1,)), ((), ()))
    lower = lax.broadcasted_iota(jnp.int32, (ROWS, ROWS), 0) >= lax.broadcasted_iota(
        jnp.int32, (ROWS, ROWS), 1
    )
    block = where_ref[0]
    mine = [x[slot, block].reshape(ROWS, PIECE) for slot in range(N_TM)]
    plain = jnp.concatenate(mine, 1)
    crossed = jnp.concatenate([x for m in mine for x in (m[:, SPEC:], -m[:, :SPEC])], 1)
    for other in range(N_TM):
        cols = slice(other * ROWS, (other + 1) * ROWS)
        left = jnp.where(other <= block, plain, crossed)
        right = jnp.concatenate(
            [x[slot, other].reshape(ROWS, PIECE) for slot in range(N_TM)], 1
        )
        part = lax.dot_general(left, right, contract, preferred_element_type=jnp.float32)
        out_ref[:, cols] = (part * scale).astype(jnp.bfloat16)
    part = lax.dot_general(crossed, plain, contract, preferred_element_type=jnp.float32)
    at = pl.ds(pl.multiple_of(block * ROWS, ROWS), ROWS)
    both = jnp.where(lower, out_ref[:, at].astype(jnp.float32), part * scale)
    out_ref[:, at] = both.astype(jnp.bfloat16)


def correlate(block, z_lo, layout, arrays):
    used = sorted({part[0] for parts in layout for part in parts})
    layout = [[(used.index(part[0]), *part[1:]) for part in parts] for parts in layout]
    arrays = [in_hbm(arrays[which]) for which in used]
    vmem = pl.BlockSpec(memory_space=pltpu.VMEM)
    where = jnp.stack([block, z_lo]).astype(jnp.int32)
    return pl.pallas_call(
        functools.partial(correlate_kernel, layout),
        in_specs=[pl.BlockSpec(memory_space=pltpu.SMEM)]
        + [pl.BlockSpec(memory_space=pltpu.HBM)] * len(arrays),
        out_specs=vmem,
        out_shape=jax.ShapeDtypeStruct((ROWS, INPUTS), jnp.bfloat16),
        scratch_shapes=[
            pltpu.VMEM((N_TM, N_TM, 2, *BLOCK[1:]), jnp.bfloat16),
            pltpu.SemaphoreType.DMA((N_Z + 1,)),
        ],
        compiler_params=params(12),
        name="correlate",
    )(where, *arrays)


def gather_kernel(position_ref, *refs):
    planes, out_ref, wide = refs[:CH_DEV], refs[CH_DEV], refs[CH_DEV + 1]
    rows = planes[0].shape[0]
    for place in range(CH_DEV):
        channel = 2 * lax.rem(position_ref[0] + place // 2, N_TM) + place % 2
        for part in range(INPUTS // 128):
            cols = slice(part * 128, (part + 1) * 128)
            wide[part, pl.ds(channel, rows, stride=CH_DEV), :] = planes[place][:, cols].astype(
                jnp.float32
            )
    for part in range(INPUTS // 128):
        cols = slice(part * 128, (part + 1) * 128)
        out_ref[:, :, cols] = wide[part].astype(jnp.bfloat16).reshape(rows, CH_DEV, 128)


def gather_planes(position, planes):
    block = 64
    return pl.pallas_call(
        gather_kernel,
        grid=(ROWS // block,),
        in_specs=[pl.BlockSpec(memory_space=pltpu.SMEM)]
        + [pl.BlockSpec((block, INPUTS), lambda g: (g, 0))] * CH_DEV,
        out_specs=pl.BlockSpec((block, CH_DEV, INPUTS), lambda g: (g, 0, 0)),
        out_shape=jax.ShapeDtypeStruct((ROWS, CH_DEV, INPUTS), jnp.bfloat16),
        scratch_shapes=[pltpu.VMEM((INPUTS // 128, block * CH_DEV, 128), jnp.float32)],
        compiler_params=params(32),
        name="gather_planes",
    )(position.astype(jnp.int32).reshape(1), *planes)


def places(which):
    at, early = 4 * which, 6 * which
    here = [(0, early), (1, 8 + at), (0, early + 1), (5, 0), (5, 4), (0, early + 2), (4, at), (2, at)]
    there = [(0, early + 3), (2, 8 + at), (0, early + 4), (1, at), (3, at), (0, early + 5), (6, 4), (6, 0)]
    return [[[(*place, 0, 4)] for place in side] for side in (here, there)]


def per_device(voltages, window, first_channel):
    position = lax.axis_index("tm")
    z_lo = lax.axis_index("feed") // 8 % 2
    z = 2 * position + z_lo
    after, before = (position + 1) % N_TM, (position + N_TM - 1) % N_TM
    carried, first_channel = lax.optimization_barrier((carry(voltages, window), first_channel))
    arrived = lax.ppermute(carried, "tm", [(i, i + 1) for i in range(N_TM - 1)])
    dft_table, window = lax.optimization_barrier((table(first_channel, z), window))
    filtered, head = filter_own(voltages, window)
    planes = [None] * CH_DEV

    dests = [[(0, 4 * i)] for i in range(FAR)]
    dests += [[(1 + i // 2, i % 2 * 4)] for i in range(2 * N_Z - FAR)]
    spectra, twos, zeros, fives = dft(filtered, head, arrived, dft_table, (4 * FAR, 8, 8, 8), dests)
    turned = turn(spectra.reshape(-1, INP, PIECE)).reshape(*BLOCK[:2], FAR, *BLOCK[2:])
    left_5, right_5 = both_ways(fives, fives, 3)
    left_2, right_0 = both_ways(twos, zeros, 2)
    early = [zeros, left_2, right_5, right_0, twos, left_5]
    everything = slice(None)
    (packed,) = move(
        early,
        [(*BLOCK[:2], 2 * len(early), *BLOCK[2:])],
        [
            (n, (pl.ds(4 * which, 4),), 0, (everything, everything, len(early) * which + n))
            for which in range(2)
            for n in range(len(early))
        ],
    )
    packed = turn(packed.reshape(-1, INP, PIECE)).reshape(packed.shape)
    sent = ((3, 1), (7, 1), (4,), (6,))
    sent_31, sent_71, sent_4, sent_6 = move(
        [turned],
        [(8 * len(deltas), *BLOCK[1:]) for deltas in sent],
        [
            (0, (everything, everything, len(LATE) * which + LATE.index(delta)), i, (pl.ds(8 * n + 4 * which, 4),))
            for i, deltas in enumerate(sent)
            for n, delta in enumerate(deltas)
            for which in range(2)
        ],
    )
    left_31, right_71 = both_ways(sent_31, sent_71, 1)
    left_4, right_6 = both_ways(sent_4, sent_6, 2)

    for which in range(2):
        here, there = places(which)
        part = slice(4 * which, 4 * which + 4)
        far = both_ways(
            jnp.concatenate([left_31[part], left_4[part]]),
            jnp.concatenate([right_71[part], right_6[part]]),
            2,
        )
        arrays = [packed, left_31, right_71, left_4, right_6, *far]
        planes[2 + which], planes[4 + which] = both_ways(
            correlate(before, z_lo, here, arrays), correlate(after, z_lo, there, arrays), 2
        )
        planes[0 + which] = correlate(position, z_lo, here, arrays)
        planes[6 + which] = correlate(position, z_lo, there, arrays)
    return gather_planes(position, planes)


def solution(mesh):
    in_specs = (P("feed", "tm"), P(), P())
    out_specs = P("tm", "feed", None)
    return jax.shard_map(
        per_device, mesh=mesh, in_specs=in_specs, out_specs=out_specs, check_vma=False
    )
```

```python
import functools
import math

import jax
import jax.numpy as jnp
from jax import lax
from jax.experimental import pallas as pl
from jax.experimental.pallas import tpu as pltpu
from jax.sharding import PartitionSpec as P

FRAME = 2048
TAPS = 4
INP = 16
SPEC = 64
INPUTS = 1024
N_TM = 4
N_FEED = 64
N_Z = 8
N_D = 32
CH_DEV = 8
FRAME_BLOCK = 8
DEPTH = 4
LANES = 256
COARSE = 32
FINE = FRAME // COARSE
ROWS = INPUTS // N_TM
PIECE = 2 * SPEC
BLOCK = (N_TM, N_D // N_TM, INP, PIECE)
EARLY = (2, 0, 5)
LATE = (1, 3, 4, 6, 7)
FAR = 2 * len(LATE)
MIB = 1 << 20


def in_hbm(x):
    return pltpu.with_memory_space_constraint(x, pltpu.HBM)


def params(mib):
    return pltpu.CompilerParams(vmem_limit_bytes=mib * MIB)


def place_of(tm, z_lo, d):
    return tm * N_FEED + (d // 8 * 2 + z_lo) * 8 + d % 8


def along_z(x, by):
    pairs = []
    for z in range(N_Z):
        to = (z + by) % N_Z
        for d in range(N_D):
            pairs.append((place_of(z // 2, z % 2, d), place_of(to // 2, to % 2, d)))
    return lax.ppermute(x, ("tm", "feed"), pairs)


def both_ways(left, right, by):
    return lax.optimization_barrier((along_z(left, -by), along_z(right, by)))


def turn(x):
    groups = [[place_of(0, z_lo, d) for d in range(N_D)] for z_lo in range(2)]
    return lax.all_to_all(
        x, "feed", split_axis=0, concat_axis=0, tiled=True, axis_index_groups=groups
    )


def carry_kernel(v_ref, w_ref, out_ref, held, sem):
    at = v_ref.shape[1] - (TAPS - 1) * FRAME
    copy = pltpu.make_async_copy(v_ref.at[:, pl.ds(at, (TAPS - 1) * FRAME)], held, sem)
    copy.start()
    copy.wait()
    for head in range(TAPS - 1):
        for start in range(0, FRAME, LANES):
            total = jnp.zeros((INP, LANES), jnp.float32)
            for tap in range(head + 1, TAPS):
                at = (TAPS - 1 + head - tap) * FRAME + start
                total = total + w_ref[tap : tap + 1, start : start + LANES] * held[
                    :, at : at + LANES
                ].astype(jnp.float32)
            out_ref[head * INP : (head + 1) * INP, start : start + LANES] = total.astype(jnp.bfloat16)


def carry(voltages, window):
    return pl.pallas_call(
        carry_kernel,
        in_specs=[
            pl.BlockSpec(memory_space=pltpu.HBM),
            pl.BlockSpec(memory_space=pltpu.VMEM),
        ],
        out_specs=pl.BlockSpec(memory_space=pltpu.VMEM),
        out_shape=jax.ShapeDtypeStruct(((TAPS - 1) * INP, FRAME), jnp.bfloat16),
        scratch_shapes=[
            pltpu.VMEM((INP, (TAPS - 1) * FRAME), jnp.int32),
            pltpu.SemaphoreType.DMA,
        ],
        compiler_params=params(8),
        name="carry",
    )(in_hbm(voltages), window)


def filter_kernel(v_ref, w_ref, out_ref, head_ref, held, past, sems):
    width = FRAME_BLOCK * FRAME
    steps = SPEC // FRAME_BLOCK

    def fetch(step):
        return pltpu.make_async_copy(
            v_ref.at[:, pl.ds(step * width, width)], held.at[step % DEPTH], sems.at[step % DEPTH]
        )

    for step in range(DEPTH - 1):
        fetch(step).start()
    past[...] = jnp.zeros_like(past)
    for step in range(steps):
        if step + DEPTH - 1 < steps:
            fetch(step + DEPTH - 1).start()
        fetch(step).wait()
        for start in range(0, FRAME, LANES):
            cols = slice(start, start + LANES)
            taps = [
                jnp.broadcast_to(w_ref[p : p + 1, cols], (INP, LANES)) for p in range(TAPS)
            ]
            seen = [past[p, :, cols] for p in range(TAPS - 1)]
            for k in range(FRAME_BLOCK):
                now = held[step % DEPTH, :, k * FRAME + start : k * FRAME + start + LANES].astype(
                    jnp.float32
                )
                total = taps[0] * now
                for p in range(1, TAPS):
                    total = total + taps[p] * seen[p - 1]
                row = (step * FRAME_BLOCK + k) * INP
                out_ref[row : row + INP, cols] = total.astype(jnp.bfloat16)
                if row < head_ref.shape[0]:
                    head_ref[row : row + INP, cols] = total
                seen = [now] + seen[:-1]
            for p in range(TAPS - 1):
                past[p, :, cols] = seen[p]


def filter_own(voltages, window):
    head_rows = (TAPS - 1) * INP
    vmem = pl.BlockSpec(memory_space=pltpu.VMEM)
    return pl.pallas_call(
        filter_kernel,
        in_specs=[pl.BlockSpec(memory_space=pltpu.HBM), vmem],
        out_specs=[vmem, vmem],
        out_shape=[
            jax.ShapeDtypeStruct((SPEC * INP, FRAME), jnp.bfloat16),
            jax.ShapeDtypeStruct((head_rows, FRAME), jnp.float32),
        ],
        scratch_shapes=[
            pltpu.VMEM((DEPTH, INP, FRAME_BLOCK * FRAME), jnp.int32),
            pltpu.VMEM((TAPS - 1, INP, FRAME), jnp.float32),
            pltpu.SemaphoreType.DMA((DEPTH,)),
        ],
        compiler_params=params(14),
        name="own_filter",
    )(in_hbm(voltages), window)


def table_kernel(coarse_cos, coarse_sin, fine_cos, fine_sin, out_ref):
    half = out_ref.shape[2] // 2
    for part in range(out_ref.shape[0]):
        cols = slice(part * half, (part + 1) * half)
        for a in range(COARSE):
            ac, as_ = coarse_cos[a : a + 1, cols], coarse_sin[a : a + 1, cols]
            bc, bs = fine_cos[:, cols], fine_sin[:, cols]
            rows = slice(a * FINE, (a + 1) * FINE)
            out_ref[part, rows, :half] = (ac * bc - as_ * bs).astype(jnp.bfloat16)
            out_ref[part, rows, half:] = (-(as_ * bc) - ac * bs).astype(jnp.bfloat16)


def table(first_channel, z):
    column = lax.iota(jnp.int32, N_D * FAR)
    runs = jnp.repeat(jnp.arange(2 * len(EARLY), dtype=jnp.int32), N_D)
    early, late = jnp.array(EARLY, jnp.int32), jnp.array(LATE, jnp.int32)
    d = jnp.concatenate([column // FAR, lax.iota(jnp.int32, N_D * 2 * len(EARLY)) % N_D])
    delta = jnp.concatenate([late[column % len(LATE)], early[runs // 2]])
    which = jnp.concatenate([column % FAR // len(LATE), runs % 2])
    group = (z + N_Z - delta) % N_Z
    feed = (d // 8 * 2 + group % 2) * 8 + d % 8
    channel = first_channel[0] + feed * CH_DEV + group // 2 * 2 + which

    def waves(samples):
        phase = samples[:, None] * channel[None, :] % FRAME
        angle = phase.astype(jnp.float32) * jnp.float32(2.0 * math.pi / FRAME)
        return jnp.cos(angle), jnp.sin(angle)

    scale = jnp.float32(1.0 / math.sqrt(FRAME))
    coarse = waves(FINE * lax.iota(jnp.int32, COARSE))
    fine = waves(lax.iota(jnp.int32, FINE))
    return pl.pallas_call(
        table_kernel,
        out_shape=jax.ShapeDtypeStruct((4, FRAME, N_D * N_Z), jnp.bfloat16),
        compiler_params=params(16),
        name="dft_table",
    )(coarse[0], coarse[1], fine[0] * scale, fine[1] * scale)


def product_kernel(f_ref, t_ref, out_ref):
    for part in range(t_ref.shape[0]):
        both = jnp.dot(f_ref[...], t_ref[part], preferred_element_type=jnp.float32)
        for r in range(2):
            out_ref[part, r] = both[:, r * 128 : (r + 1) * 128]


def product(filtered, dft_table):
    vmem = pl.BlockSpec(memory_space=pltpu.VMEM)
    return pl.pallas_call(
        product_kernel,
        in_specs=[vmem] * 2,
        out_specs=vmem,
        out_shape=jax.ShapeDtypeStruct((dft_table.shape[0], 2, SPEC * INP, 128), jnp.float32),
        compiler_params=params(12),
        name="product",
    )(filtered, dft_table)


def dft_kernel(dests, position_ref, wide, head_ref, arrived_ref, t_ref, *refs):
    outs, (heads, turned) = refs[:-2], refs[-2:]
    head_rows = head_ref.shape[0]
    arrived = jnp.where(position_ref[0] > 0, arrived_ref[...].astype(jnp.float32), 0.0)
    fixed = (head_ref[...] + arrived).astype(jnp.bfloat16)
    for part in range(t_ref.shape[0]):
        first = jnp.dot(fixed, t_ref[part], preferred_element_type=jnp.float32)
        for r in range(2):
            heads[part, r, :head_rows, :] = first[:, r * 128 : (r + 1) * 128]
    is_head = lax.broadcasted_iota(jnp.int32, (8, 128), 0) < TAPS - 1
    for part in range(t_ref.shape[0]):
        for i in range(INP):
            frames = []
            for r in range(2):
                top, rest = pl.ds(i, 8, stride=INP), pl.ds(i + 8 * INP, SPEC - 8, stride=INP)
                frames.append(jnp.where(is_head, heads[part, r, top, :], wide[part, r, top, :]))
                frames.append(wide[part, r, rest, :])
            turned[part, pl.ds(i, 128, stride=INP), :] = jnp.concatenate(frames, 0).T
        for run in range(4):
            rows = slice(run * N_D * INP, (run + 1) * N_D * INP)
            block = turned[part, rows, :].astype(jnp.bfloat16).reshape(BLOCK)
            for which, at in dests[part * 4 + run]:
                outs[which][at : at + 4] = block


def dft(position, wide, head, arrived, dft_table, counts, dests):
    parts = dft_table.shape[0]
    vmem = pl.BlockSpec(memory_space=pltpu.VMEM)
    return pl.pallas_call(
        functools.partial(dft_kernel, dests),
        in_specs=[pl.BlockSpec(memory_space=pltpu.SMEM)] + [vmem] * 4,
        out_specs=[vmem] * len(counts),
        out_shape=[jax.ShapeDtypeStruct((count, *BLOCK[1:]), jnp.bfloat16) for count in counts],
        scratch_shapes=[
            pltpu.VMEM((parts, 2, 8 * INP, 128), jnp.float32),
            pltpu.VMEM((parts, 128 * INP, PIECE), jnp.float32),
        ],
        compiler_params=params(16),
        name="dft",
    )(position, wide, head, arrived, dft_table)


def move_kernel(moves, n_in, *refs):
    ins, outs, sems = refs[:n_in], refs[n_in:-1], refs[-1]
    copies = [
        pltpu.make_async_copy(ins[i].at[src], outs[o].at[dst], sems.at[n])
        for n, (i, src, o, dst) in enumerate(moves)
    ]
    for copy in copies:
        copy.start()
    for copy in copies:
        copy.wait()


def move(arrays, shapes, moves):
    return pl.pallas_call(
        functools.partial(move_kernel, moves, len(arrays)),
        in_specs=[pl.BlockSpec(memory_space=pltpu.HBM)] * len(arrays),
        out_specs=[pl.BlockSpec(memory_space=pltpu.VMEM)] * len(shapes),
        out_shape=[jax.ShapeDtypeStruct(shape, jnp.bfloat16) for shape in shapes],
        scratch_shapes=[pltpu.SemaphoreType.DMA((len(moves),))],
        compiler_params=params(4),
        name="move",
    )(*[in_hbm(x) for x in arrays])


def correlate_kernel(layout, where_ref, *refs):
    arrays, (out_ref, x, sems) = refs[:-3], refs[-3:]
    z_lo = where_ref[1]
    copies = []
    for delta, parts in enumerate(layout):
        step, odd = divmod(delta, 2)
        half = lax.rem(z_lo + odd, 2)
        slot = lax.rem(step + z_lo * odd, N_TM)
        for which, at, to, count in parts:
            if len(arrays[which].shape) == 5:
                source = arrays[which].at[:, :, at]
            else:
                source = arrays[which].at[pl.ds(at, count)]
            goal = x.at[slot, pl.ds(to, count), half]
            copies.append(pltpu.make_async_copy(source, goal, sems.at[len(copies)]))
    for copy in copies:
        copy.start()
    for copy in copies:
        copy.wait()
    scale = jnp.float32(1.0 / (SPEC * N_TM))
    contract = (((1,), (1,)), ((), ()))
    lower = lax.broadcasted_iota(jnp.int32, (ROWS, ROWS), 0) >= lax.broadcasted_iota(
        jnp.int32, (ROWS, ROWS), 1
    )
    block = where_ref[0]
    mine = [x[slot, block].reshape(ROWS, PIECE) for slot in range(N_TM)]
    plain = jnp.concatenate(mine, 1)
    crossed = jnp.concatenate([x for m in mine for x in (m[:, SPEC:], -m[:, :SPEC])], 1)
    for other in range(N_TM):
        cols = slice(other * ROWS, (other + 1) * ROWS)
        left = jnp.where(other <= block, plain, crossed)
        right = jnp.concatenate(
            [x[slot, other].reshape(ROWS, PIECE) for slot in range(N_TM)], 1
        )
        part = lax.dot_general(left, right, contract, preferred_element_type=jnp.float32)
        out_ref[:, cols] = (part * scale).astype(jnp.bfloat16)
    part = lax.dot_general(crossed, plain, contract, preferred_element_type=jnp.float32)
    at = pl.ds(pl.multiple_of(block * ROWS, ROWS), ROWS)
    both = jnp.where(lower, out_ref[:, at].astype(jnp.float32), part * scale)
    out_ref[:, at] = both.astype(jnp.bfloat16)


def correlate(block, z_lo, layout, arrays):
    used = sorted({part[0] for parts in layout for part in parts})
    layout = [[(used.index(part[0]), *part[1:]) for part in parts] for parts in layout]
    arrays = [in_hbm(arrays[which]) for which in used]
    vmem = pl.BlockSpec(memory_space=pltpu.VMEM)
    where = jnp.stack([block, z_lo]).astype(jnp.int32)
    return pl.pallas_call(
        functools.partial(correlate_kernel, layout),
        in_specs=[pl.BlockSpec(memory_space=pltpu.SMEM)]
        + [pl.BlockSpec(memory_space=pltpu.HBM)] * len(arrays),
        out_specs=vmem,
        out_shape=jax.ShapeDtypeStruct((ROWS, INPUTS), jnp.bfloat16),
        scratch_shapes=[
            pltpu.VMEM((N_TM, N_TM, 2, *BLOCK[1:]), jnp.bfloat16),
            pltpu.SemaphoreType.DMA((N_Z + 1,)),
        ],
        compiler_params=params(12),
        name="correlate",
    )(where, *arrays)


def gather_kernel(position_ref, *refs):
    planes, out_ref, wide = refs[:CH_DEV], refs[CH_DEV], refs[CH_DEV + 1]
    rows = planes[0].shape[0]
    for place in range(CH_DEV):
        channel = 2 * lax.rem(position_ref[0] + place // 2, N_TM) + place % 2
        for part in range(INPUTS // 128):
            cols = slice(part * 128, (part + 1) * 128)
            wide[part, pl.ds(channel, rows, stride=CH_DEV), :] = planes[place][:, cols].astype(
                jnp.float32
            )
    for part in range(INPUTS // 128):
        cols = slice(part * 128, (part + 1) * 128)
        out_ref[:, :, cols] = wide[part].astype(jnp.bfloat16).reshape(rows, CH_DEV, 128)


def gather_planes(position, planes):
    block = 64
    return pl.pallas_call(
        gather_kernel,
        grid=(ROWS // block,),
        in_specs=[pl.BlockSpec(memory_space=pltpu.SMEM)]
        + [pl.BlockSpec((block, INPUTS), lambda g: (g, 0))] * CH_DEV,
        out_specs=pl.BlockSpec((block, CH_DEV, INPUTS), lambda g: (g, 0, 0)),
        out_shape=jax.ShapeDtypeStruct((ROWS, CH_DEV, INPUTS), jnp.bfloat16),
        scratch_shapes=[pltpu.VMEM((INPUTS // 128, block * CH_DEV, 128), jnp.float32)],
        compiler_params=params(32),
        name="gather_planes",
    )(position.astype(jnp.int32).reshape(1), *planes)


def places(which):
    at, early = 4 * which, 6 * which
    here = [(0, early), (1, 8 + at), (0, early + 1), (5, 0), (5, 4), (0, early + 2), (4, at), (2, at)]
    there = [(0, early + 3), (2, 8 + at), (0, early + 4), (1, at), (3, at), (0, early + 5), (6, 4), (6, 0)]
    return [[[(*place, 0, 4)] for place in side] for side in (here, there)]


def per_device(voltages, window, first_channel):
    position = lax.axis_index("tm")
    z_lo = lax.axis_index("feed") // 8 % 2
    z = 2 * position + z_lo
    after, before = (position + 1) % N_TM, (position + N_TM - 1) % N_TM
    carried, first_channel = lax.optimization_barrier((carry(voltages, window), first_channel))
    arrived = along_z(carried, 2)
    where = position.astype(jnp.int32).reshape(1)
    dft_table, window, where = lax.optimization_barrier((table(first_channel, z), window, where))
    filtered, head = filter_own(voltages, window)
    planes = [None] * CH_DEV

    dests = [[(0, 4 * i)] for i in range(FAR)]
    dests += [[(1 + i // 2, i % 2 * 4)] for i in range(2 * N_Z - FAR)]
    spectra, twos, zeros, fives = dft(
        where, product(filtered, dft_table), head, arrived, dft_table, (4 * FAR, 8, 8, 8), dests
    )
    turned = turn(spectra.reshape(-1, INP, PIECE)).reshape(*BLOCK[:2], FAR, *BLOCK[2:])
    left_5, right_5 = both_ways(fives, fives, 3)
    left_2, right_0 = both_ways(twos, zeros, 2)
    early = [zeros, left_2, right_5, right_0, twos, left_5]
    everything = slice(None)
    (packed,) = move(
        early,
        [(*BLOCK[:2], 2 * len(early), *BLOCK[2:])],
        [
            (n, (pl.ds(4 * which, 4),), 0, (everything, everything, len(early) * which + n))
            for which in range(2)
            for n in range(len(early))
        ],
    )
    packed = turn(packed.reshape(-1, INP, PIECE)).reshape(packed.shape)
    sent = ((3, 1), (7, 1), (4,), (6,))
    sent_31, sent_71, sent_4, sent_6 = move(
        [turned],
        [(8 * len(deltas), *BLOCK[1:]) for deltas in sent],
        [
            (0, (everything, everything, len(LATE) * which + LATE.index(delta)), i, (pl.ds(8 * n + 4 * which, 4),))
            for i, deltas in enumerate(sent)
            for n, delta in enumerate(deltas)
            for which in range(2)
        ],
    )
    left_31, right_71 = both_ways(sent_31, sent_71, 1)
    left_4, right_6 = both_ways(sent_4, sent_6, 2)

    def onward(which):
        part = slice(4 * which, 4 * which + 4)
        return [
            jnp.concatenate([left_31[part], left_4[part]]),
            jnp.concatenate([right_71[part], right_6[part]]),
        ]

    far_0 = both_ways(*onward(0), 2)
    far_0, onward_1 = lax.optimization_barrier((far_0, onward(1)))
    far_1 = both_ways(*onward_1, 2)
    for which, far in enumerate((far_0, far_1)):
        here, there = places(which)
        arrays = [packed, left_31, right_71, left_4, right_6, *far]
        planes[2 + which], planes[4 + which] = both_ways(
            correlate(before, z_lo, here, arrays), correlate(after, z_lo, there, arrays), 2
        )
        planes[0 + which] = correlate(position, z_lo, here, arrays)
        planes[6 + which] = correlate(position, z_lo, there, arrays)
    return gather_planes(position, planes)


def solution(mesh):
    in_specs = (P("feed", "tm"), P(), P())
    out_specs = P("tm", "feed", None)
    return jax.shard_map(
        per_device, mesh=mesh, in_specs=in_specs, out_specs=out_specs, check_vma=False
    )
```

```python
import functools
import math

import jax
import jax.numpy as jnp
from jax import lax
from jax.experimental import pallas as pl
from jax.experimental.pallas import tpu as pltpu
from jax.sharding import PartitionSpec as P

FRAME = 2048
TAPS = 4
INP = 16
SPEC = 64
INPUTS = 1024
N_TM = 4
N_FEED = 64
N_Z = 8
N_D = 32
CH_DEV = 8
FRAME_BLOCK = 8
DEPTH = 4
LANES = 256
COARSE = 32
FINE = FRAME // COARSE
ROWS = INPUTS // N_TM
PIECE = 2 * SPEC
BLOCK = (N_TM, N_D // N_TM, INP, PIECE)
EARLY = (2, 0, 5)
LATE = (1, 3, 4, 6, 7)
FAR = 2 * len(LATE)
MIB = 1 << 20


def in_hbm(x):
    return pltpu.with_memory_space_constraint(x, pltpu.HBM)


def params(mib):
    return pltpu.CompilerParams(vmem_limit_bytes=mib * MIB)


def place_of(tm, z_lo, d):
    return tm * N_FEED + (d // 8 * 2 + z_lo) * 8 + d % 8


def along_z(x, by):
    pairs = []
    for z in range(N_Z):
        to = (z + by) % N_Z
        for d in range(N_D):
            pairs.append((place_of(z // 2, z % 2, d), place_of(to // 2, to % 2, d)))
    return lax.ppermute(x, ("tm", "feed"), pairs)


def both_ways(left, right, by):
    return lax.optimization_barrier((along_z(left, -by), along_z(right, by)))


def turn(x):
    groups = [[place_of(0, z_lo, d) for d in range(N_D)] for z_lo in range(2)]
    return lax.all_to_all(
        x, "feed", split_axis=0, concat_axis=0, tiled=True, axis_index_groups=groups
    )


def carry_kernel(v_ref, w_ref, out_ref, held, sem):
    at = v_ref.shape[1] - (TAPS - 1) * FRAME
    copy = pltpu.make_async_copy(v_ref.at[:, pl.ds(at, (TAPS - 1) * FRAME)], held, sem)
    copy.start()
    copy.wait()
    for head in range(TAPS - 1):
        for start in range(0, FRAME, LANES):
            total = jnp.zeros((INP, LANES), jnp.float32)
            for tap in range(head + 1, TAPS):
                at = (TAPS - 1 + head - tap) * FRAME + start
                total = total + w_ref[tap : tap + 1, start : start + LANES] * held[
                    :, at : at + LANES
                ].astype(jnp.float32)
            out_ref[head * INP : (head + 1) * INP, start : start + LANES] = total.astype(jnp.bfloat16)


def carry(voltages, window):
    return pl.pallas_call(
        carry_kernel,
        in_specs=[
            pl.BlockSpec(memory_space=pltpu.HBM),
            pl.BlockSpec(memory_space=pltpu.VMEM),
        ],
        out_specs=pl.BlockSpec(memory_space=pltpu.VMEM),
        out_shape=jax.ShapeDtypeStruct(((TAPS - 1) * INP, FRAME), jnp.bfloat16),
        scratch_shapes=[
            pltpu.VMEM((INP, (TAPS - 1) * FRAME), jnp.int32),
            pltpu.SemaphoreType.DMA,
        ],
        compiler_params=params(8),
        name="carry",
    )(in_hbm(voltages), window)


def filter_kernel(v_ref, w_ref, out_ref, head_ref, held, past, sems):
    width = FRAME_BLOCK * FRAME
    steps = SPEC // FRAME_BLOCK

    def fetch(step):
        return pltpu.make_async_copy(
            v_ref.at[:, pl.ds(step * width, width)], held.at[step % DEPTH], sems.at[step % DEPTH]
        )

    for step in range(DEPTH - 1):
        fetch(step).start()
    past[...] = jnp.zeros_like(past)
    for step in range(steps):
        if step + DEPTH - 1 < steps:
            fetch(step + DEPTH - 1).start()
        fetch(step).wait()
        for start in range(0, FRAME, LANES):
            cols = slice(start, start + LANES)
            taps = [
                jnp.broadcast_to(w_ref[p : p + 1, cols], (INP, LANES)) for p in range(TAPS)
            ]
            seen = [past[p, :, cols] for p in range(TAPS - 1)]
            for k in range(FRAME_BLOCK):
                now = held[step % DEPTH, :, k * FRAME + start : k * FRAME + start + LANES].astype(
                    jnp.float32
                )
                total = taps[0] * now
                for p in range(1, TAPS):
                    total = total + taps[p] * seen[p - 1]
                row = (step * FRAME_BLOCK + k) * INP
                out_ref[row : row + INP, cols] = total.astype(jnp.bfloat16)
                if row < head_ref.shape[0]:
                    head_ref[row : row + INP, cols] = total
                seen = [now] + seen[:-1]
            for p in range(TAPS - 1):
                past[p, :, cols] = seen[p]


def filter_own(voltages, window):
    head_rows = (TAPS - 1) * INP
    vmem = pl.BlockSpec(memory_space=pltpu.VMEM)
    return pl.pallas_call(
        filter_kernel,
        in_specs=[pl.BlockSpec(memory_space=pltpu.HBM), vmem],
        out_specs=[vmem, vmem],
        out_shape=[
            jax.ShapeDtypeStruct((SPEC * INP, FRAME), jnp.bfloat16),
            jax.ShapeDtypeStruct((head_rows, FRAME), jnp.float32),
        ],
        scratch_shapes=[
            pltpu.VMEM((DEPTH, INP, FRAME_BLOCK * FRAME), jnp.int32),
            pltpu.VMEM((TAPS - 1, INP, FRAME), jnp.float32),
            pltpu.SemaphoreType.DMA((DEPTH,)),
        ],
        compiler_params=params(14),
        name="own_filter",
    )(in_hbm(voltages), window)


def table_kernel(coarse_cos, coarse_sin, fine_cos, fine_sin, out_ref):
    half = out_ref.shape[2] // 2
    for part in range(out_ref.shape[0]):
        cols = slice(part * half, (part + 1) * half)
        for a in range(COARSE):
            ac, as_ = coarse_cos[a : a + 1, cols], coarse_sin[a : a + 1, cols]
            bc, bs = fine_cos[:, cols], fine_sin[:, cols]
            rows = slice(a * FINE, (a + 1) * FINE)
            out_ref[part, rows, :half] = (ac * bc - as_ * bs).astype(jnp.bfloat16)
            out_ref[part, rows, half:] = (-(as_ * bc) - ac * bs).astype(jnp.bfloat16)


def table(first_channel, z):
    column = lax.iota(jnp.int32, N_D * FAR)
    runs = jnp.repeat(jnp.arange(2 * len(EARLY), dtype=jnp.int32), N_D)
    early, late = jnp.array(EARLY, jnp.int32), jnp.array(LATE, jnp.int32)
    d = jnp.concatenate([column // FAR, lax.iota(jnp.int32, N_D * 2 * len(EARLY)) % N_D])
    delta = jnp.concatenate([late[column % len(LATE)], early[runs // 2]])
    which = jnp.concatenate([column % FAR // len(LATE), runs % 2])
    group = (z + N_Z - delta) % N_Z
    feed = (d // 8 * 2 + group % 2) * 8 + d % 8
    channel = first_channel[0] + feed * CH_DEV + group // 2 * 2 + which

    def waves(samples):
        phase = samples[:, None] * channel[None, :] % FRAME
        angle = phase.astype(jnp.float32) * jnp.float32(2.0 * math.pi / FRAME)
        return jnp.cos(angle), jnp.sin(angle)

    scale = jnp.float32(1.0 / math.sqrt(FRAME))
    coarse = waves(FINE * lax.iota(jnp.int32, COARSE))
    fine = waves(lax.iota(jnp.int32, FINE))
    return pl.pallas_call(
        table_kernel,
        out_shape=jax.ShapeDtypeStruct((4, FRAME, N_D * N_Z), jnp.bfloat16),
        compiler_params=params(16),
        name="dft_table",
    )(coarse[0], coarse[1], fine[0] * scale, fine[1] * scale)


def product_kernel(f_ref, t_ref, out_ref):
    for part in range(t_ref.shape[0]):
        both = jnp.dot(f_ref[...], t_ref[part], preferred_element_type=jnp.float32)
        for r in range(2):
            out_ref[part, r] = both[:, r * 128 : (r + 1) * 128]


def product(filtered, dft_table):
    vmem = pl.BlockSpec(memory_space=pltpu.VMEM)
    return pl.pallas_call(
        product_kernel,
        in_specs=[vmem] * 2,
        out_specs=vmem,
        out_shape=jax.ShapeDtypeStruct((dft_table.shape[0], 2, SPEC * INP, 128), jnp.float32),
        compiler_params=params(12),
        name="product",
    )(filtered, dft_table)


def dft_kernel(dests, position_ref, wide, head_ref, arrived_ref, t_ref, *refs):
    outs, (heads, turned) = refs[:-2], refs[-2:]
    head_rows = head_ref.shape[0]
    arrived = jnp.where(position_ref[0] > 0, arrived_ref[...].astype(jnp.float32), 0.0)
    fixed = (head_ref[...] + arrived).astype(jnp.bfloat16)
    for part in range(t_ref.shape[0]):
        first = jnp.dot(fixed, t_ref[part], preferred_element_type=jnp.float32)
        for r in range(2):
            heads[part, r, :head_rows, :] = first[:, r * 128 : (r + 1) * 128]
    is_head = lax.broadcasted_iota(jnp.int32, (8, 128), 0) < TAPS - 1
    for part in range(t_ref.shape[0]):
        for i in range(INP):
            frames = []
            for r in range(2):
                top, rest = pl.ds(i, 8, stride=INP), pl.ds(i + 8 * INP, SPEC - 8, stride=INP)
                frames.append(jnp.where(is_head, heads[part, r, top, :], wide[part, r, top, :]))
                frames.append(wide[part, r, rest, :])
            turned[part, pl.ds(i, 128, stride=INP), :] = jnp.concatenate(frames, 0).T
        for run in range(4):
            rows = slice(run * N_D * INP, (run + 1) * N_D * INP)
            block = turned[part, rows, :].astype(jnp.bfloat16).reshape(BLOCK)
            for which, at in dests[part * 4 + run]:
                outs[which][at : at + 4] = block


def dft(position, wide, head, arrived, dft_table, counts, dests):
    parts = dft_table.shape[0]
    vmem = pl.BlockSpec(memory_space=pltpu.VMEM)
    return pl.pallas_call(
        functools.partial(dft_kernel, dests),
        in_specs=[pl.BlockSpec(memory_space=pltpu.SMEM)] + [vmem] * 4,
        out_specs=[vmem] * len(counts),
        out_shape=[jax.ShapeDtypeStruct((count, *BLOCK[1:]), jnp.bfloat16) for count in counts],
        scratch_shapes=[
            pltpu.VMEM((parts, 2, 8 * INP, 128), jnp.float32),
            pltpu.VMEM((parts, 128 * INP, PIECE), jnp.float32),
        ],
        compiler_params=params(16),
        name="dft",
    )(position, wide, head, arrived, dft_table)


def move_kernel(moves, n_in, *refs):
    ins, outs, sems = refs[:n_in], refs[n_in:-1], refs[-1]
    copies = [
        pltpu.make_async_copy(ins[i].at[src], outs[o].at[dst], sems.at[n])
        for n, (i, src, o, dst) in enumerate(moves)
    ]
    for copy in copies:
        copy.start()
    for copy in copies:
        copy.wait()


def move(arrays, shapes, moves):
    return pl.pallas_call(
        functools.partial(move_kernel, moves, len(arrays)),
        in_specs=[pl.BlockSpec(memory_space=pltpu.HBM)] * len(arrays),
        out_specs=[pl.BlockSpec(memory_space=pltpu.VMEM)] * len(shapes),
        out_shape=[jax.ShapeDtypeStruct(shape, jnp.bfloat16) for shape in shapes],
        scratch_shapes=[pltpu.SemaphoreType.DMA((len(moves),))],
        compiler_params=params(4),
        name="move",
    )(*[in_hbm(x) for x in arrays])


def correlate_kernel(layout, where_ref, *refs):
    arrays, (out_ref, x, sems) = refs[:-3], refs[-3:]
    z_lo = where_ref[1]
    copies = []
    for delta, parts in enumerate(layout):
        step, odd = divmod(delta, 2)
        half = lax.rem(z_lo + odd, 2)
        slot = lax.rem(step + z_lo * odd, N_TM)
        for which, at, to, count in parts:
            if len(arrays[which].shape) == 5:
                source = arrays[which].at[:, :, at]
            else:
                source = arrays[which].at[pl.ds(at, count)]
            goal = x.at[slot, pl.ds(to, count), half]
            copies.append(pltpu.make_async_copy(source, goal, sems.at[len(copies)]))
    for copy in copies:
        copy.start()
    for copy in copies:
        copy.wait()
    scale = jnp.float32(1.0 / (SPEC * N_TM))
    contract = (((1,), (1,)), ((), ()))
    lower = lax.broadcasted_iota(jnp.int32, (ROWS, ROWS), 0) >= lax.broadcasted_iota(
        jnp.int32, (ROWS, ROWS), 1
    )
    block = where_ref[0]
    mine = [x[slot, block].reshape(ROWS, PIECE) for slot in range(N_TM)]
    plain = jnp.concatenate(mine, 1)
    crossed = jnp.concatenate([x for m in mine for x in (m[:, SPEC:], -m[:, :SPEC])], 1)
    for other in range(N_TM):
        cols = slice(other * ROWS, (other + 1) * ROWS)
        left = jnp.where(other <= block, plain, crossed)
        right = jnp.concatenate(
            [x[slot, other].reshape(ROWS, PIECE) for slot in range(N_TM)], 1
        )
        part = lax.dot_general(left, right, contract, preferred_element_type=jnp.float32)
        out_ref[:, cols] = (part * scale).astype(jnp.bfloat16)
    part = lax.dot_general(crossed, plain, contract, preferred_element_type=jnp.float32)
    at = pl.ds(pl.multiple_of(block * ROWS, ROWS), ROWS)
    both = jnp.where(lower, out_ref[:, at].astype(jnp.float32), part * scale)
    out_ref[:, at] = both.astype(jnp.bfloat16)


def correlate(block, z_lo, layout, arrays):
    used = sorted({part[0] for parts in layout for part in parts})
    layout = [[(used.index(part[0]), *part[1:]) for part in parts] for parts in layout]
    arrays = [in_hbm(arrays[which]) for which in used]
    vmem = pl.BlockSpec(memory_space=pltpu.VMEM)
    where = jnp.stack([block, z_lo]).astype(jnp.int32)
    return pl.pallas_call(
        functools.partial(correlate_kernel, layout),
        in_specs=[pl.BlockSpec(memory_space=pltpu.SMEM)]
        + [pl.BlockSpec(memory_space=pltpu.HBM)] * len(arrays),
        out_specs=vmem,
        out_shape=jax.ShapeDtypeStruct((ROWS, INPUTS), jnp.bfloat16),
        scratch_shapes=[
            pltpu.VMEM((N_TM, N_TM, 2, *BLOCK[1:]), jnp.bfloat16),
            pltpu.SemaphoreType.DMA((N_Z + 1,)),
        ],
        compiler_params=params(12),
        name="correlate",
    )(where, *arrays)


def gather_kernel(position_ref, *refs):
    planes, out_ref, wide = refs[:CH_DEV], refs[CH_DEV], refs[CH_DEV + 1]
    rows = planes[0].shape[0]
    for place in range(CH_DEV):
        channel = 2 * lax.rem(position_ref[0] + place // 2, N_TM) + place % 2
        for part in range(INPUTS // 128):
            cols = slice(part * 128, (part + 1) * 128)
            wide[part, pl.ds(channel, rows, stride=CH_DEV), :] = planes[place][:, cols].astype(
                jnp.float32
            )
    for part in range(INPUTS // 128):
        cols = slice(part * 128, (part + 1) * 128)
        out_ref[:, :, cols] = wide[part].astype(jnp.bfloat16).reshape(rows, CH_DEV, 128)


def gather_planes(position, planes):
    block = 64
    return pl.pallas_call(
        gather_kernel,
        grid=(ROWS // block,),
        in_specs=[pl.BlockSpec(memory_space=pltpu.SMEM)]
        + [pl.BlockSpec((block, INPUTS), lambda g: (g, 0))] * CH_DEV,
        out_specs=pl.BlockSpec((block, CH_DEV, INPUTS), lambda g: (g, 0, 0)),
        out_shape=jax.ShapeDtypeStruct((ROWS, CH_DEV, INPUTS), jnp.bfloat16),
        scratch_shapes=[pltpu.VMEM((INPUTS // 128, block * CH_DEV, 128), jnp.float32)],
        compiler_params=params(32),
        name="gather_planes",
    )(position.astype(jnp.int32).reshape(1), *planes)


def places(which):
    at, early = 4 * which, 6 * which
    here = [(0, early), (7, at), (0, early + 1), (5, 0), (5, 4), (0, early + 2), (4, at), (2, at)]
    there = [(0, early + 3), (8, at), (0, early + 4), (1, at), (3, at), (0, early + 5), (6, 4), (6, 0)]
    return [[[(*place, 0, 4)] for place in side] for side in (here, there)]


def per_device(voltages, window, first_channel):
    position = lax.axis_index("tm")
    z_lo = lax.axis_index("feed") // 8 % 2
    z = 2 * position + z_lo
    after, before = (position + 1) % N_TM, (position + N_TM - 1) % N_TM
    carried, first_channel = lax.optimization_barrier((carry(voltages, window), first_channel))
    arrived = along_z(carried, 2)
    where = position.astype(jnp.int32).reshape(1)
    dft_table, window, where = lax.optimization_barrier((table(first_channel, z), window, where))
    filtered, head = filter_own(voltages, window)
    planes = [None] * CH_DEV

    dests = [[(0, 4 * i)] for i in range(FAR)]
    dests += [[(1 + i // 2, i % 2 * 4)] for i in range(2 * N_Z - FAR)]
    spectra, twos, zeros, fives = dft(
        where, product(filtered, dft_table), head, arrived, dft_table, (4 * FAR, 8, 8, 8), dests
    )
    turned = turn(spectra.reshape(-1, INP, PIECE)).reshape(*BLOCK[:2], FAR, *BLOCK[2:])
    left_5, right_5 = both_ways(fives, fives, 3)
    left_2, right_0 = both_ways(twos, zeros, 2)
    early = [zeros, left_2, right_5, right_0, twos, left_5]
    everything = slice(None)
    (packed,) = move(
        early,
        [(*BLOCK[:2], 2 * len(early), *BLOCK[2:])],
        [
            (n, (pl.ds(4 * which, 4),), 0, (everything, everything, len(early) * which + n))
            for which in range(2)
            for n in range(len(early))
        ],
    )
    packed = turn(packed.reshape(-1, INP, PIECE)).reshape(packed.shape)
    sent = ((3,), (7,), (4,), (6,), (1,))
    sent_3, sent_7, sent_4, sent_6, sent_1 = move(
        [turned],
        [(8 * len(deltas), *BLOCK[1:]) for deltas in sent],
        [
            (0, (everything, everything, len(LATE) * which + LATE.index(delta)), i, (pl.ds(8 * n + 4 * which, 4),))
            for i, deltas in enumerate(sent)
            for n, delta in enumerate(deltas)
            for which in range(2)
        ],
    )
    left_31, right_71 = both_ways(sent_3, sent_7, 1)
    left_4, right_6 = both_ways(sent_4, sent_6, 2)
    sent_1, left_4, right_6 = lax.optimization_barrier((sent_1, left_4, right_6))
    ones = both_ways(sent_1, sent_1, 1)

    def onward(which):
        part = slice(4 * which, 4 * which + 4)
        return [
            jnp.concatenate([left_31[part], left_4[part]]),
            jnp.concatenate([right_71[part], right_6[part]]),
        ]

    far_0 = both_ways(*onward(0), 2)
    far_0, onward_1 = lax.optimization_barrier((far_0, onward(1)))
    far_1 = both_ways(*onward_1, 2)
    for which, far in enumerate((far_0, far_1)):
        here, there = places(which)
        arrays = [packed, left_31, right_71, left_4, right_6, *far, *ones]
        planes[2 + which], planes[4 + which] = both_ways(
            correlate(before, z_lo, here, arrays), correlate(after, z_lo, there, arrays), 2
        )
        planes[0 + which] = correlate(position, z_lo, here, arrays)
        planes[6 + which] = correlate(position, z_lo, there, arrays)
    return gather_planes(position, planes)


def solution(mesh):
    in_specs = (P("feed", "tm"), P(), P())
    out_specs = P("tm", "feed", None)
    return jax.shard_map(
        per_device, mesh=mesh, in_specs=in_specs, out_specs=out_specs, check_vma=False
    )
```

```python
import functools
import math

import jax
import jax.numpy as jnp
from jax import lax
from jax.experimental import pallas as pl
from jax.experimental.pallas import tpu as pltpu
from jax.sharding import PartitionSpec as P

FRAME = 2048
TAPS = 4
INP = 16
SPEC = 64
INPUTS = 1024
N_TM = 4
N_FEED = 64
N_Z = 8
N_D = 32
CH_DEV = 8
FRAME_BLOCK = 8
DEPTH = 4
LANES = 256
COARSE = 32
FINE = FRAME // COARSE
ROWS = INPUTS // N_TM
PIECE = 2 * SPEC
BLOCK = (N_TM, N_D // N_TM, INP, PIECE)
EARLY = (2, 0, 5)
LATE = (1, 3, 4, 6, 7)
FAR = 2 * len(LATE)
MIB = 1 << 20


def in_hbm(x):
    return pltpu.with_memory_space_constraint(x, pltpu.HBM)


def params(mib):
    return pltpu.CompilerParams(vmem_limit_bytes=mib * MIB)


def place_of(tm, z_lo, d):
    return tm * N_FEED + (d // 8 * 2 + z_lo) * 8 + d % 8


def along_z(x, by):
    pairs = []
    for z in range(N_Z):
        to = (z + by) % N_Z
        for d in range(N_D):
            pairs.append((place_of(z // 2, z % 2, d), place_of(to // 2, to % 2, d)))
    return lax.ppermute(x, ("tm", "feed"), pairs)


def both_ways(left, right, by):
    return lax.optimization_barrier((along_z(left, -by), along_z(right, by)))


def turn(x):
    groups = [[place_of(0, z_lo, d) for d in range(N_D)] for z_lo in range(2)]
    return lax.all_to_all(
        x, "feed", split_axis=0, concat_axis=0, tiled=True, axis_index_groups=groups
    )


def carry_kernel(v_ref, w_ref, out_ref, held, sem):
    at = v_ref.shape[1] - (TAPS - 1) * FRAME
    copy = pltpu.make_async_copy(v_ref.at[:, pl.ds(at, (TAPS - 1) * FRAME)], held, sem)
    copy.start()
    copy.wait()
    for head in range(TAPS - 1):
        for start in range(0, FRAME, LANES):
            total = jnp.zeros((INP, LANES), jnp.float32)
            for tap in range(head + 1, TAPS):
                at = (TAPS - 1 + head - tap) * FRAME + start
                total = total + w_ref[tap : tap + 1, start : start + LANES] * held[
                    :, at : at + LANES
                ].astype(jnp.float32)
            out_ref[head * INP : (head + 1) * INP, start : start + LANES] = total.astype(jnp.bfloat16)


def carry(voltages, window):
    return pl.pallas_call(
        carry_kernel,
        in_specs=[
            pl.BlockSpec(memory_space=pltpu.HBM),
            pl.BlockSpec(memory_space=pltpu.VMEM),
        ],
        out_specs=pl.BlockSpec(memory_space=pltpu.VMEM),
        out_shape=jax.ShapeDtypeStruct(((TAPS - 1) * INP, FRAME), jnp.bfloat16),
        scratch_shapes=[
            pltpu.VMEM((INP, (TAPS - 1) * FRAME), jnp.int32),
            pltpu.SemaphoreType.DMA,
        ],
        compiler_params=params(8),
        name="carry",
    )(in_hbm(voltages), window)


def filter_kernel(v_ref, w_ref, out_ref, head_ref, held, past, sems):
    width = FRAME_BLOCK * FRAME
    steps = SPEC // FRAME_BLOCK

    def fetch(step):
        return pltpu.make_async_copy(
            v_ref.at[:, pl.ds(step * width, width)], held.at[step % DEPTH], sems.at[step % DEPTH]
        )

    for step in range(DEPTH - 1):
        fetch(step).start()
    past[...] = jnp.zeros_like(past)
    for step in range(steps):
        if step + DEPTH - 1 < steps:
            fetch(step + DEPTH - 1).start()
        fetch(step).wait()
        for start in range(0, FRAME, LANES):
            cols = slice(start, start + LANES)
            taps = [
                jnp.broadcast_to(w_ref[p : p + 1, cols], (INP, LANES)) for p in range(TAPS)
            ]
            seen = [past[p, :, cols] for p in range(TAPS - 1)]
            for k in range(FRAME_BLOCK):
                now = held[step % DEPTH, :, k * FRAME + start : k * FRAME + start + LANES].astype(
                    jnp.float32
                )
                total = taps[0] * now
                for p in range(1, TAPS):
                    total = total + taps[p] * seen[p - 1]
                row = (step * FRAME_BLOCK + k) * INP
                out_ref[row : row + INP, cols] = total.astype(jnp.bfloat16)
                if row < head_ref.shape[0]:
                    head_ref[row : row + INP, cols] = total
                seen = [now] + seen[:-1]
            for p in range(TAPS - 1):
                past[p, :, cols] = seen[p]


def filter_own(voltages, window):
    head_rows = (TAPS - 1) * INP
    vmem = pl.BlockSpec(memory_space=pltpu.VMEM)
    return pl.pallas_call(
        filter_kernel,
        in_specs=[pl.BlockSpec(memory_space=pltpu.HBM), vmem],
        out_specs=[vmem, vmem],
        out_shape=[
            jax.ShapeDtypeStruct((SPEC * INP, FRAME), jnp.bfloat16),
            jax.ShapeDtypeStruct((head_rows, FRAME), jnp.float32),
        ],
        scratch_shapes=[
            pltpu.VMEM((DEPTH, INP, FRAME_BLOCK * FRAME), jnp.int32),
            pltpu.VMEM((TAPS - 1, INP, FRAME), jnp.float32),
            pltpu.SemaphoreType.DMA((DEPTH,)),
        ],
        compiler_params=params(14),
        name="own_filter",
    )(in_hbm(voltages), window)


def table_kernel(coarse_cos, coarse_sin, fine_cos, fine_sin, out_ref):
    half = out_ref.shape[2] // 2
    for part in range(out_ref.shape[0]):
        cols = slice(part * half, (part + 1) * half)
        for a in range(COARSE):
            ac, as_ = coarse_cos[a : a + 1, cols], coarse_sin[a : a + 1, cols]
            bc, bs = fine_cos[:, cols], fine_sin[:, cols]
            rows = slice(a * FINE, (a + 1) * FINE)
            out_ref[part, rows, :half] = (ac * bc - as_ * bs).astype(jnp.bfloat16)
            out_ref[part, rows, half:] = (-(as_ * bc) - ac * bs).astype(jnp.bfloat16)


def table(first_channel, z):
    column = lax.iota(jnp.int32, N_D * FAR)
    runs = jnp.repeat(jnp.arange(2 * len(EARLY), dtype=jnp.int32), N_D)
    early, late = jnp.array(EARLY, jnp.int32), jnp.array(LATE, jnp.int32)
    d = jnp.concatenate([column // FAR, lax.iota(jnp.int32, N_D * 2 * len(EARLY)) % N_D])
    delta = jnp.concatenate([late[column % len(LATE)], early[runs // 2]])
    which = jnp.concatenate([column % FAR // len(LATE), runs % 2])
    group = (z + N_Z - delta) % N_Z
    feed = (d // 8 * 2 + group % 2) * 8 + d % 8
    channel = first_channel[0] + feed * CH_DEV + group // 2 * 2 + which

    def waves(samples):
        phase = samples[:, None] * channel[None, :] % FRAME
        angle = phase.astype(jnp.float32) * jnp.float32(2.0 * math.pi / FRAME)
        return jnp.cos(angle), jnp.sin(angle)

    scale = jnp.float32(1.0 / math.sqrt(FRAME))
    coarse = waves(FINE * lax.iota(jnp.int32, COARSE))
    fine = waves(lax.iota(jnp.int32, FINE))
    return pl.pallas_call(
        table_kernel,
        out_shape=jax.ShapeDtypeStruct((4, FRAME, N_D * N_Z), jnp.bfloat16),
        compiler_params=params(16),
        name="dft_table",
    )(coarse[0], coarse[1], fine[0] * scale, fine[1] * scale)


def product_kernel(f_ref, t_ref, out_ref):
    for part in range(t_ref.shape[0]):
        both = jnp.dot(f_ref[...], t_ref[part], preferred_element_type=jnp.float32)
        for r in range(2):
            out_ref[part, r] = both[:, r * 128 : (r + 1) * 128]


def product(filtered, dft_table):
    vmem = pl.BlockSpec(memory_space=pltpu.VMEM)
    return pl.pallas_call(
        product_kernel,
        in_specs=[vmem] * 2,
        out_specs=vmem,
        out_shape=jax.ShapeDtypeStruct((dft_table.shape[0], 2, SPEC * INP, 128), jnp.float32),
        compiler_params=params(12),
        name="product",
    )(filtered, dft_table)


def dft_kernel(dests, position_ref, wide, head_ref, arrived_ref, t_ref, *refs):
    outs, (heads, turned) = refs[:-2], refs[-2:]
    head_rows = head_ref.shape[0]
    arrived = jnp.where(position_ref[0] > 0, arrived_ref[...].astype(jnp.float32), 0.0)
    fixed = (head_ref[...] + arrived).astype(jnp.bfloat16)
    for part in range(t_ref.shape[0]):
        first = jnp.dot(fixed, t_ref[part], preferred_element_type=jnp.float32)
        for r in range(2):
            heads[part, r, :head_rows, :] = first[:, r * 128 : (r + 1) * 128]
    is_head = lax.broadcasted_iota(jnp.int32, (8, 128), 0) < TAPS - 1
    for part in range(t_ref.shape[0]):
        for i in range(INP):
            frames = []
            for r in range(2):
                top, rest = pl.ds(i, 8, stride=INP), pl.ds(i + 8 * INP, SPEC - 8, stride=INP)
                frames.append(jnp.where(is_head, heads[part, r, top, :], wide[part, r, top, :]))
                frames.append(wide[part, r, rest, :])
            turned[part, pl.ds(i, 128, stride=INP), :] = jnp.concatenate(frames, 0).T
        for run in range(4):
            rows = slice(run * N_D * INP, (run + 1) * N_D * INP)
            block = turned[part, rows, :].astype(jnp.bfloat16).reshape(BLOCK)
            for which, at in dests[part * 4 + run]:
                outs[which][at : at + 4] = block


def dft(position, wide, head, arrived, dft_table, counts, dests):
    parts = dft_table.shape[0]
    vmem = pl.BlockSpec(memory_space=pltpu.VMEM)
    return pl.pallas_call(
        functools.partial(dft_kernel, dests),
        in_specs=[pl.BlockSpec(memory_space=pltpu.SMEM)] + [vmem] * 4,
        out_specs=[vmem] * len(counts),
        out_shape=[jax.ShapeDtypeStruct((count, *BLOCK[1:]), jnp.bfloat16) for count in counts],
        scratch_shapes=[
            pltpu.VMEM((parts, 2, 8 * INP, 128), jnp.float32),
            pltpu.VMEM((parts, 128 * INP, PIECE), jnp.float32),
        ],
        compiler_params=params(16),
        name="dft",
    )(position, wide, head, arrived, dft_table)


def move_kernel(moves, n_in, *refs):
    ins, outs, sems = refs[:n_in], refs[n_in:-1], refs[-1]
    copies = [
        pltpu.make_async_copy(ins[i].at[src], outs[o].at[dst], sems.at[n])
        for n, (i, src, o, dst) in enumerate(moves)
    ]
    for copy in copies:
        copy.start()
    for copy in copies:
        copy.wait()


def move(arrays, shapes, moves):
    return pl.pallas_call(
        functools.partial(move_kernel, moves, len(arrays)),
        in_specs=[pl.BlockSpec(memory_space=pltpu.HBM)] * len(arrays),
        out_specs=[pl.BlockSpec(memory_space=pltpu.VMEM)] * len(shapes),
        out_shape=[jax.ShapeDtypeStruct(shape, jnp.bfloat16) for shape in shapes],
        scratch_shapes=[pltpu.SemaphoreType.DMA((len(moves),))],
        compiler_params=params(4),
        name="move",
    )(*[in_hbm(x) for x in arrays])


def correlate_kernel(layout, where_ref, *refs):
    arrays, (out_ref, x, sems) = refs[:-3], refs[-3:]
    z_lo = where_ref[1]
    copies = []
    for delta, parts in enumerate(layout):
        step, odd = divmod(delta, 2)
        half = lax.rem(z_lo + odd, 2)
        slot = lax.rem(step + z_lo * odd, N_TM)
        for which, at, to, count in parts:
            if len(arrays[which].shape) == 5:
                source = arrays[which].at[:, :, at]
            else:
                source = arrays[which].at[pl.ds(at, count)]
            goal = x.at[slot, pl.ds(to, count), half]
            copies.append(pltpu.make_async_copy(source, goal, sems.at[len(copies)]))
    for copy in copies:
        copy.start()
    for copy in copies:
        copy.wait()
    scale = jnp.float32(1.0 / (SPEC * N_TM))
    contract = (((1,), (1,)), ((), ()))
    lower = lax.broadcasted_iota(jnp.int32, (ROWS, ROWS), 0) >= lax.broadcasted_iota(
        jnp.int32, (ROWS, ROWS), 1
    )
    block = where_ref[0]
    mine = [x[slot, block].reshape(ROWS, PIECE) for slot in range(N_TM)]
    plain = jnp.concatenate(mine, 1)
    crossed = jnp.concatenate([x for m in mine for x in (m[:, SPEC:], -m[:, :SPEC])], 1)
    for other in range(N_TM):
        cols = slice(other * ROWS, (other + 1) * ROWS)
        left = jnp.where(other <= block, plain, crossed)
        right = jnp.concatenate(
            [x[slot, other].reshape(ROWS, PIECE) for slot in range(N_TM)], 1
        )
        part = lax.dot_general(left, right, contract, preferred_element_type=jnp.float32)
        out_ref[:, cols] = (part * scale).astype(jnp.bfloat16)
    part = lax.dot_general(crossed, plain, contract, preferred_element_type=jnp.float32)
    at = pl.ds(pl.multiple_of(block * ROWS, ROWS), ROWS)
    both = jnp.where(lower, out_ref[:, at].astype(jnp.float32), part * scale)
    out_ref[:, at] = both.astype(jnp.bfloat16)


def correlate(block, z_lo, layout, arrays):
    used = sorted({part[0] for parts in layout for part in parts})
    layout = [[(used.index(part[0]), *part[1:]) for part in parts] for parts in layout]
    arrays = [in_hbm(arrays[which]) for which in used]
    vmem = pl.BlockSpec(memory_space=pltpu.VMEM)
    where = jnp.stack([block, z_lo]).astype(jnp.int32)
    return pl.pallas_call(
        functools.partial(correlate_kernel, layout),
        in_specs=[pl.BlockSpec(memory_space=pltpu.SMEM)]
        + [pl.BlockSpec(memory_space=pltpu.HBM)] * len(arrays),
        out_specs=vmem,
        out_shape=jax.ShapeDtypeStruct((ROWS, INPUTS), jnp.bfloat16),
        scratch_shapes=[
            pltpu.VMEM((N_TM, N_TM, 2, *BLOCK[1:]), jnp.bfloat16),
            pltpu.SemaphoreType.DMA((N_Z + 1,)),
        ],
        compiler_params=params(12),
        name="correlate",
    )(where, *arrays)


def gather_kernel(position_ref, *refs):
    planes, out_ref, wide = refs[:CH_DEV], refs[CH_DEV], refs[CH_DEV + 1]
    rows = planes[0].shape[0]
    for place in range(CH_DEV):
        channel = 2 * lax.rem(position_ref[0] + place // 2, N_TM) + place % 2
        for part in range(INPUTS // 128):
            cols = slice(part * 128, (part + 1) * 128)
            wide[part, pl.ds(channel, rows, stride=CH_DEV), :] = planes[place][:, cols].astype(
                jnp.float32
            )
    for part in range(INPUTS // 128):
        cols = slice(part * 128, (part + 1) * 128)
        out_ref[:, :, cols] = wide[part].astype(jnp.bfloat16).reshape(rows, CH_DEV, 128)


def gather_planes(position, planes):
    block = 64
    return pl.pallas_call(
        gather_kernel,
        grid=(ROWS // block,),
        in_specs=[pl.BlockSpec(memory_space=pltpu.SMEM)]
        + [pl.BlockSpec((block, INPUTS), lambda g: (g, 0))] * CH_DEV,
        out_specs=pl.BlockSpec((block, CH_DEV, INPUTS), lambda g: (g, 0, 0)),
        out_shape=jax.ShapeDtypeStruct((ROWS, CH_DEV, INPUTS), jnp.bfloat16),
        scratch_shapes=[pltpu.VMEM((INPUTS // 128, block * CH_DEV, 128), jnp.float32)],
        compiler_params=params(32),
        name="gather_planes",
    )(position.astype(jnp.int32).reshape(1), *planes)


def places(which):
    at, early = 4 * which, 6 * which
    here = [(0, early), (7, 0), (0, early + 1), (5, 0), (5, 4), (0, early + 2), (4, at), (2, at)]
    there = [(0, early + 3), (8, 0), (0, early + 4), (1, at), (3, at), (0, early + 5), (6, 4), (6, 0)]
    return [[[(*place, 0, 4)] for place in side] for side in (here, there)]


def per_device(voltages, window, first_channel):
    position = lax.axis_index("tm")
    z_lo = lax.axis_index("feed") // 8 % 2
    z = 2 * position + z_lo
    after, before = (position + 1) % N_TM, (position + N_TM - 1) % N_TM
    carried, first_channel = lax.optimization_barrier((carry(voltages, window), first_channel))
    arrived = along_z(carried, 2)
    where = position.astype(jnp.int32).reshape(1)
    dft_table, window, where = lax.optimization_barrier((table(first_channel, z), window, where))
    filtered, head = filter_own(voltages, window)
    planes = [None] * CH_DEV

    dests = [[(0, 4 * i)] for i in range(FAR)]
    dests += [[(1 + i // 2, i % 2 * 4)] for i in range(2 * N_Z - FAR)]
    spectra, twos, zeros, fives = dft(
        where, product(filtered, dft_table), head, arrived, dft_table, (4 * FAR, 8, 8, 8), dests
    )
    turned = turn(spectra.reshape(-1, INP, PIECE)).reshape(*BLOCK[:2], FAR, *BLOCK[2:])
    left_5, right_5 = both_ways(fives, fives, 3)
    left_2, right_0 = both_ways(twos, zeros, 2)
    early = [zeros, left_2, right_5, right_0, twos, left_5]
    everything = slice(None)
    (packed,) = move(
        early,
        [(*BLOCK[:2], 2 * len(early), *BLOCK[2:])],
        [
            (n, (pl.ds(4 * which, 4),), 0, (everything, everything, len(early) * which + n))
            for which in range(2)
            for n in range(len(early))
        ],
    )
    packed = turn(packed.reshape(-1, INP, PIECE)).reshape(packed.shape)
    sent = ((3,), (7,), (4,), (6,), (1,))
    sent_3, sent_7, sent_4, sent_6, sent_1 = move(
        [turned],
        [(8 * len(deltas), *BLOCK[1:]) for deltas in sent],
        [
            (0, (everything, everything, len(LATE) * which + LATE.index(delta)), i, (pl.ds(8 * n + 4 * which, 4),))
            for i, deltas in enumerate(sent)
            for n, delta in enumerate(deltas)
            for which in range(2)
        ],
    )
    left_31, right_71 = both_ways(sent_3, sent_7, 1)
    left_4, right_6 = both_ways(sent_4, sent_6, 2)
    sent_1, left_4, right_6 = lax.optimization_barrier((sent_1, left_4, right_6))
    ones = [both_ways(sent_1[:4], sent_1[:4], 1)]

    def onward(which):
        part = slice(4 * which, 4 * which + 4)
        return [
            jnp.concatenate([left_31[part], left_4[part]]),
            jnp.concatenate([right_71[part], right_6[part]]),
        ]

    far_0 = both_ways(*onward(0), 2)
    far_0, onward_1, sent_1 = lax.optimization_barrier((far_0, onward(1), sent_1))
    far_1 = both_ways(*onward_1, 2)
    ones.append(both_ways(sent_1[4:], sent_1[4:], 1))
    for which, far in enumerate((far_0, far_1)):
        here, there = places(which)
        arrays = [packed, left_31, right_71, left_4, right_6, *far, *ones[which]]
        planes[2 + which], planes[4 + which] = both_ways(
            correlate(before, z_lo, here, arrays), correlate(after, z_lo, there, arrays), 2
        )
        planes[0 + which] = correlate(position, z_lo, here, arrays)
        planes[6 + which] = correlate(position, z_lo, there, arrays)
    return gather_planes(position, planes)


def solution(mesh):
    in_specs = (P("feed", "tm"), P(), P())
    out_specs = P("tm", "feed", None)
    return jax.shard_map(
        per_device, mesh=mesh, in_specs=in_specs, out_specs=out_specs, check_vma=False
    )
```
